128 devices in a mesh: mom: 16 (over z, y), hist: 8 (over x, core).
Axes of the slice: x: 4, y: 4, z: 4, core: 2. Of those that a mesh axis runs over, the one named last changes fastest.
Arguments:
- greens: bfloat16 [2, 64, 1024, 1024], P(None, 'hist', 'mom'), may hold values from -6 to 6
- advanced: bfloat16 [2, 1024, 64, 1024], P(None, 'mom', 'hist'), may hold values from -1 to 1
- coupling: float32 [1024], P('mom'), may hold values from 0.3 to 1
- bounds: int32 [8], replicated, may hold values from 1 to 64, as said below
Outputs:
- collision: float32 [8, 2, 1024, 1024], P('hist', None, 'mom')
The draws below stay inside these ranges and needn't reach their ends.
Inputs may be any that keep to these rules, and one draw needn't show every extreme that they name: `bounds`: every draw has some target time index whose memory covers all 64 stored steps.
All inputs are finite; a program needn't handle non-finite values.
Results may differ from the reference program's by a relative error of at most 0.012.
Values may be sent and summed in bfloat16 or wider, within the bound.
A program may use at most 128 MiB of HBM per device.

```python
import math
import jax
import jax.numpy as jnp
from jax import lax

L = 32
NO = 32
K = 1024
NS = 64
NT = 8


def draw_bounds(key, part):
    key = jax.random.fold_in(key, 5)
    first_key, second_key = jax.random.split(key)
    values = jax.random.randint(first_key, (NT,), 1, NS + 1)
    chosen = jax.random.randint(second_key, (), 0, NT)
    values = jnp.where(jnp.arange(NT) == chosen, NS, values)
    return values.astype(jnp.int32)


def shard_levels(rng, extent, shards, low, largest):
    def one(axis_at, parts):
        draws = jax.random.uniform(jax.random.fold_in(jax.random.fold_in(rng, 6), axis_at), (parts,), jnp.float32, low / len(shards), largest / len(shards))
        return jnp.repeat(jnp.exp(draws), extent[axis_at] // parts).reshape((-1,) + (1,) * (len(extent) - axis_at - 1))

    loudness = one(*shards[0])
    for cut in shards[1:]:
        loudness = loudness * one(*cut)
    return loudness


def gaussian(rng, extent, spread, reach, pieces=(), kind=jnp.bfloat16):
    drawn = jax.random.normal(rng, extent, jnp.float32) * spread
    if len(pieces) > 0:
        drawn = shard_levels(rng, extent, pieces, -0.22, 0.18) * drawn
    return jnp.clip(drawn, min=-reach, max=reach).astype(kind)


def setup_inputs(seed: int = 0) -> dict:
    seeds = jax.random.split(jax.random.key(seed), 5)
    greens = gaussian(seeds[0], (2, NS, K, NO * NO), 1.0, 6.0, ((1, 8), (2, 16)))
    advanced = gaussian(seeds[1], (2, K, NS, NO * NO), NO ** -0.5, 1.0, ((1, 16), (2, 8)))
    coupling = jnp.clip(jnp.exp(math.log(1.0) - 1.2039728 * jax.random.uniform(seeds[2], (NO * NO,), jnp.float32) ** shard_levels(seeds[2], (NO * NO,), ((0, 16),), -0.2, 0.2)), 0.3, 1.0)
    bounds = draw_bounds(jax.random.fold_in(seeds[4], 71), 0)
    return dict(greens=greens, advanced=advanced, coupling=coupling, bounds=bounds)


def make_tables(size):
    index = jnp.arange(size, dtype=jnp.int32)
    phase = index[:, None] * index[None, :] % size
    angle = phase.astype(jnp.float32) * (2.0 * math.pi / size)
    norm = 1.0 / math.sqrt(size)
    return ((jnp.cos(angle) * norm).astype(jnp.bfloat16), (jnp.sin(angle) * norm).astype(jnp.bfloat16))

def apply_table(table, data, pattern):
    return jnp.einsum(pattern, table.astype(jnp.float32), data.astype(jnp.float32), precision=lax.Precision.HIGHEST)

def rotate(real_part, imag_part, cosines, sines, pattern, sign):
    new_real = apply_table(cosines, real_part, pattern) - sign * apply_table(sines, imag_part, pattern)
    new_imag = apply_table(cosines, imag_part, pattern) + sign * apply_table(sines, real_part, pattern)
    return (new_real, new_imag)

def self_energy(grid, weight, cosines, sines):
    along_x = 'xm,smyp->sxyp'
    along_y = 'yn,sxnp->sxyp'
    first_re, first_im = rotate(grid[0], grid[1], cosines, sines, along_x, 1.0)
    first_re = first_re.astype(jnp.bfloat16)
    first_im = first_im.astype(jnp.bfloat16)
    space_re, space_im = rotate(first_re, first_im, cosines, sines, along_y, 1.0)
    mirror_re = jnp.roll(jnp.flip(space_re, (1, 2)), 1, (1, 2))
    mirror_im = jnp.roll(jnp.flip(space_im, (1, 2)), 1, (1, 2))
    square_re = space_re * space_re - space_im * space_im
    square_im = 2.0 * space_re * space_im
    sigma_re = (weight * (square_re * mirror_re + square_im * mirror_im)).astype(jnp.bfloat16)
    sigma_im = (weight * (square_im * mirror_re - square_re * mirror_im)).astype(jnp.bfloat16)
    back_re, back_im = rotate(sigma_re, sigma_im, cosines, sines, along_y, -1.0)
    back_re = back_re.astype(jnp.bfloat16)
    back_im = back_im.astype(jnp.bfloat16)
    final_re, final_im = rotate(back_re, back_im, cosines, sines, along_x, -1.0)
    return jnp.stack([final_re.astype(jnp.bfloat16), final_im.astype(jnp.bfloat16)])

def reference(greens, advanced, coupling, bounds):
    cosines, sines = make_tables(L)
    weight = coupling * coupling

    def one_step(pair):
        green_step, adv_step = pair
        grid = green_step.reshape(2, 1, L, L, NO * NO)
        sigma = self_energy(grid, weight, cosines, sines).reshape(2, L * L, NO, NO).astype(jnp.float32)
        right = adv_step.reshape(2, L * L, NO, NO).astype(jnp.float32)
        prod_re = jnp.einsum('kac,kcb->kab', sigma[0], right[0], precision=lax.Precision.HIGHEST) - jnp.einsum('kac,kcb->kab', sigma[1], right[1], precision=lax.Precision.HIGHEST)
        prod_im = jnp.einsum('kac,kcb->kab', sigma[0], right[1], precision=lax.Precision.HIGHEST) + jnp.einsum('kac,kcb->kab', sigma[1], right[0], precision=lax.Precision.HIGHEST)
        return jnp.stack([prod_re, prod_im]).reshape(2, L * L, NO * NO)
    products = lax.map(one_step, (jnp.transpose(greens, (1, 0, 2, 3)), jnp.transpose(advanced, (2, 0, 1, 3))))
    spots = jnp.arange(NS, dtype=jnp.int32)
    mask = (spots[None, :] < bounds[:, None]).astype(jnp.float32) * (1.0 / math.sqrt(NS))
    return jnp.einsum('js,sxkp->jxkp', mask, products, precision=lax.Precision.HIGHEST)
```

```python
import functools
import math

import jax
import jax.numpy as jnp
import ml_dtypes
import numpy as np
from jax import lax
from jax.experimental import pallas as pl
from jax.experimental.pallas import tpu as pltpu
from jax.sharding import PartitionSpec as P

MESH = pl.DeviceIdType.MESH
L = 32
NO = 32
LANES = 128
CHUNKS = 8
MOM = 16
HIST = 8
STEPS = 8
KDEV = 64
GROUPS = 4
AHEAD = 3
BACK = 2
LAST = 2


def tables():
    index = np.arange(L, dtype=np.int32)
    phase = index[:, None] * index[None, :] % L
    angle = phase.astype(np.float32) * np.float32(2.0 * math.pi / L)
    norm = np.float32(1.0 / math.sqrt(L))
    cosines = (np.cos(angle) * norm).astype(ml_dtypes.bfloat16).astype(np.float32)
    sines = (np.sin(angle) * norm).astype(ml_dtypes.bfloat16).astype(np.float32)
    ahead = np.array([[cosines, -sines], [sines, cosines]])
    back = np.array([[cosines, sines], [-sines, cosines]])
    eye = np.eye(2, dtype=np.float32)
    group = np.array([[0, 16]] + [[m, L - m] for m in range(1, MOM)])
    flip = (-index) % L
    pairs = np.arange(L).reshape(MOM, 2)

    first = np.einsum("ridyk,st,lm->dsyrlitmk", ahead[:, :, group, :].reshape(2, 2, MOM, 2, L), eye, eye)
    along = ahead[:, :, :, pairs]
    space = np.einsum("rixdl,st,yw->rsyxdtwil", along, eye, eye)
    turned = along[:, :, flip]
    mirror = np.einsum("rixdl,st,yw->rsyxdtwil", turned, eye, eye[::-1])
    mirror_own = np.einsum("rixdl,st,yw->rsyxdtwil", turned, eye, eye)
    third = np.einsum("ridlx,st,yw->dsyrlitwx", back[:, :, pairs, :], eye, eye)
    last = np.einsum("rikdy,st,lm->rslkdtyim", back[:, :, :, group], eye, eye)
    square = lambda a: a.reshape(256, 256)
    moved = [np.concatenate([square(space), square(m)]) for m in (mirror, mirror_own)]
    return (
        np.stack([square(first), square(third), square(last)]).astype(ml_dtypes.bfloat16),
        np.stack(moved).astype(ml_dtypes.bfloat16),
    )


def other(me, d):
    return lax.rem(me // 4 + d // 4, 4) * 4 + lax.rem(lax.rem(me, 4) + d % 4, 4)


def kernel(
    greens, advanced, coupling, bounds, tabs, space_tab, out,
    gbuf, abuf, tbuf, sbuf, bbuf, own_c, all_c, masks,
    s1, r1, s2, r2, rows, bt, at, acc, cs, cr, obuf,
    in_sem, load_sem, c_send, c_recv, s1_send, r1_recv, s2_send, r2_recv, cs_send, cr_recv, o_sem,
):
    me = lax.axis_index("mom")
    h = lax.axis_index("hist")

    def lanes(c):
        return pl.ds(pl.multiple_of(c * LANES, LANES), LANES)

    pick = jnp.where(me == 0, 1, 0)
    tab_copy = pltpu.make_async_copy(tabs, tbuf, load_sem.at[0])
    space_copy = pltpu.make_async_copy(space_tab.at[pick], sbuf, load_sem.at[1])
    adv_copy = pltpu.make_async_copy(advanced, abuf, load_sem.at[2])
    bound_copy = pltpu.make_async_copy(bounds, bbuf, load_sem.at[3])

    def green_copy(c):
        return pltpu.make_async_copy(greens.at[:, :, :, lanes(c)], gbuf.at[c], in_sem.at[c])

    tab_copy.start()
    green_copy(0).start()
    green_copy(1).start()
    space_copy.start()
    bound_copy.start()

    barrier = pltpu.get_barrier_semaphore()
    for d in range(1, MOM):
        pl.semaphore_signal(barrier, inc=1, device_id=(other(me, d), h), device_id_type=MESH)
    for d in range(1, HIST):
        pl.semaphore_signal(barrier, inc=1, device_id=(me, lax.rem(h + d, HIST)), device_id_type=MESH)

    for c in range(2, CHUNKS):
        green_copy(c).start()
    adv_copy.start()

    def exchange(src, dst, send, recv, c):
        for d in range(1, MOM):
            p = other(me, d)
            pltpu.make_async_remote_copy(
                src_ref=src.at[c, p], dst_ref=dst.at[c, me], send_sem=send.at[c], recv_sem=recv.at[c],
                device_id=(p, h), device_id_type=MESH,
            ).start()
        dst[c, me] = src[c, me]

    def arrivals(src, dst, send, recv, c):
        return pltpu.make_async_remote_copy(
            src_ref=src.at[c, pl.ds(0, MOM - 1)], dst_ref=dst.at[c, pl.ds(0, MOM - 1)],
            send_sem=send.at[c], recv_sem=recv.at[c], device_id=(other(me, 1), h), device_id_type=MESH,
        )

    def coupling_copy(p):
        return pltpu.make_async_remote_copy(
            src_ref=own_c, dst_ref=all_c.at[me], send_sem=c_send, recv_sem=c_recv,
            device_id=(p, h), device_id_type=MESH,
        )

    def coupling_all():
        return pltpu.make_async_remote_copy(
            src_ref=all_c.at[pl.ds(0, MOM - 1)], dst_ref=all_c.at[pl.ds(0, MOM - 1)], send_sem=c_send, recv_sem=c_recv,
            device_id=(other(me, 1), h), device_id_type=MESH,
        )

    def partial_all(c):
        return pltpu.make_async_remote_copy(
            src_ref=cs.at[c, pl.ds(0, HIST - 1)], dst_ref=cr.at[c, pl.ds(0, HIST - 1)],
            send_sem=cs_send.at[c], recv_sem=cr_recv.at[c], device_id=(me, lax.rem(h + 1, HIST)), device_id_type=MESH,
        )

    def two(load, q):
        return jnp.concatenate([load(2 * q), load(2 * q + 1)], axis=1)

    def spread(dst, c, q, value):
        value = value.astype(jnp.bfloat16)
        for n in range(2):
            part = value[:, n * LANES:(n + 1) * LANES].reshape(MOM, 16, LANES)
            dst[c, :, pl.ds((2 * q + n) * 16, 16), :] = part

    def gathered(src, c):
        return lambda g: src[c, :, pl.ds(g * 16, 16), :].reshape(256, LANES)

    def forward(c):
        green_copy(c).wait()
        for q in range(2):
            data = two(lambda g: gbuf[c, :, pl.ds(2 * g, 2)].reshape(256, LANES), q)
            spread(s1, c, q, jnp.dot(tbuf[0], data, preferred_element_type=jnp.float32))

    def middle(c):
        arrivals(s1, r1, s1_send, r1_recv, c).wait_recv()
        low = lax.broadcasted_iota(jnp.int32, (1, LANES), 1) < LANES // 2
        weight = jnp.where(low, all_c[2 * c, 0:1, :], all_c[2 * c + 1, 0:1, :])
        weight = weight * weight
        weight = jnp.concatenate([weight, weight], axis=1)
        for q in range(2):
            data = two(gathered(r1, c), q)
            space = jnp.dot(sbuf[...], data, preferred_element_type=jnp.float32)
            re, im, mre, mim = (space[n * 128:(n + 1) * 128] for n in range(4))
            square_re = re * re - im * im
            square_im = 2.0 * re * im
            sigma_re = weight * (square_re * mre + square_im * mim)
            sigma_im = weight * (square_im * mre - square_re * mim)
            sigma = jnp.concatenate([sigma_re.astype(jnp.bfloat16), sigma_im.astype(jnp.bfloat16)], axis=0)
            spread(s2, c, q, jnp.dot(tbuf[1], sigma, preferred_element_type=jnp.float32))

    def products(c):
        arrivals(s2, r2, s2_send, r2_recv, c).wait_recv()
        for q in range(2):
            final = jnp.dot(tbuf[2], two(gathered(r2, c), q), preferred_element_type=jnp.float32)
            for n in range(2):
                for part in range(2):
                    block = final[part * 128:(part + 1) * 128, n * LANES:(n + 1) * LANES]
                    at[2 * q + n, part] = block.T

        def one_group(g, carry):
            def one_orbital(m, sums):
                b_re = bt[g, 0, pl.ds(pl.multiple_of(m * NO, NO), NO), :]
                b_im = bt[g, 1, pl.ds(pl.multiple_of(m * NO, NO), NO), :]
                result = []
                for a in range(4):
                    a_re = at[g, 0, pl.ds(a * NO + m, 1), :]
                    a_im = at[g, 1, pl.ds(a * NO + m, 1), :]
                    result.append(sums[2 * a] + a_re * b_re - a_im * b_im)
                    result.append(sums[2 * a + 1] + a_re * b_im + a_im * b_re)
                return tuple(result)

            zero = jnp.zeros((NO, LANES), jnp.float32)
            sums = lax.fori_loop(0, NO, one_orbital, (zero,) * 8, unroll=4)
            for a in range(4):
                acc[g, 0, pl.ds(a * NO, NO), :] = sums[2 * a]
                acc[g, 1, pl.ds(a * NO, NO), :] = sums[2 * a + 1]
            return carry

        lax.fori_loop(0, GROUPS, one_group, 0)

        def one_target(j, carry):
            low = lax.broadcasted_iota(jnp.int32, (NO, LANES), 1) < LANES // 2
            for a in range(4):
                total_re = total_im = None
                for g in range(GROUPS):
                    mask = masks[j, g, 0:1, :]
                    term_re = acc[g, 0, pl.ds(a * NO, NO), :] * mask
                    term_im = acc[g, 1, pl.ds(a * NO, NO), :] * mask
                    total_re = term_re if g == 0 else total_re + term_re
                    total_im = term_im if g == 0 else total_im + term_im
                kept = jnp.where(low, total_re, total_im)
                moved = pltpu.roll(jnp.where(low, total_im, total_re), LANES // 2, 1)
                cs[c, j, pl.ds(a * NO, NO), :] = (kept + moved).astype(jnp.bfloat16)
            return carry

        lax.fori_loop(0, HIST, one_target, 0)
        for d in range(1, HIST):
            p = lax.rem(h + d, HIST)
            pltpu.make_async_remote_copy(
                src_ref=cs.at[c, p], dst_ref=cr.at[c, h], send_sem=cs_send.at[c], recv_sem=cr_recv.at[c],
                device_id=(me, p), device_id_type=MESH,
            ).start()

    def out_copy(c):
        return pltpu.make_async_copy(obuf.at[c], out.at[0, :, :, lanes(c)], o_sem.at[c])

    def finish(c):
        partial_all(c).wait_recv()
        total = cs[c, h].astype(jnp.float32)
        for d in range(1, HIST):
            total = total + cr[c, lax.rem(h + d, HIST)].astype(jnp.float32)
        obuf[c] = total.T.reshape(2, KDEV, LANES)
        out_copy(c).start()

    def prepare_masks():
        bound_copy.wait()
        half = lax.broadcasted_iota(jnp.int32, (8, LANES), 1) // (LANES // 2)
        for j in range(HIST):
            for g in range(GROUPS):
                step = h * STEPS + 2 * g + half
                masks[j, g] = jnp.where(step < bbuf[j], 1.0 / math.sqrt(STEPS * HIST), 0.0).astype(jnp.float32)

    def prepare_advanced():
        adv_copy.wait()

        def one(n, carry):
            part, t = n // CHUNKS, lax.rem(n, CHUNKS)
            block = abuf[part, :, :, lanes(t)].astype(jnp.float32)
            rows[...] = block.reshape(KDEV * STEPS, LANES)
            for g in range(GROUPS):
                square = jnp.concatenate([rows[pl.ds(2 * g + s, KDEV, STEPS), :] for s in range(2)], axis=0)
                bt[g, part, pl.ds(pl.multiple_of(t * LANES, LANES), LANES), :] = square.T
            return carry

        lax.fori_loop(0, 2 * CHUNKS, one, 0)

    pair = coupling[...].reshape(1, KDEV)
    own_c[...] = jnp.broadcast_to(jnp.concatenate([pair, pair], axis=1), (8, LANES))
    all_c[me] = own_c[...]
    tab_copy.wait()
    forward(0)
    pl.semaphore_wait(barrier, MOM - 1 + HIST - 1)
    for d in range(1, MOM):
        coupling_copy(other(me, d)).start()
    exchange(s1, r1, s1_send, r1_recv, 0)

    def send_ahead(c, carry):
        forward(c)
        exchange(s1, r1, s1_send, r1_recv, c)
        return carry

    lax.fori_loop(1, AHEAD, send_ahead, 0)
    prepare_masks()
    prepare_advanced()
    space_copy.wait()
    coupling_all().wait_recv()

    def step(i, carry):
        @pl.when(i < CHUNKS)
        def _():
            middle(i)
            exchange(s2, r2, s2_send, r2_recv, i)

        @pl.when(i + AHEAD < CHUNKS)
        def _():
            send_ahead(i + AHEAD, 0)

        @pl.when((i >= BACK) & (i < CHUNKS + BACK))
        def _():
            products(i - BACK)

        @pl.when(i >= BACK + LAST)
        def _():
            finish(i - BACK - LAST)

        return carry

    lax.fori_loop(0, CHUNKS + BACK + LAST, step, 0)

    def drain(c, carry):
        arrivals(s1, r1, s1_send, r1_recv, c).wait_send()
        arrivals(s2, r2, s2_send, r2_recv, c).wait_send()
        partial_all(c).wait_send()
        out_copy(c).wait()
        return carry

    coupling_all().wait_send()
    lax.fori_loop(0, CHUNKS, drain, 0)


def per_device(greens, advanced, coupling, bounds):
    tabs, space_tab = tables()
    any_spec = pl.BlockSpec(memory_space=pl.ANY)
    bf16, f32 = jnp.bfloat16, jnp.float32
    dma = pltpu.SemaphoreType.DMA
    blocks = pltpu.VMEM((CHUNKS, MOM, 64, LANES), bf16)
    parts = pltpu.VMEM((CHUNKS, HIST, LANES, LANES), bf16)
    return pl.pallas_call(
        kernel,
        out_shape=jax.ShapeDtypeStruct((1, 2, KDEV, NO * NO), f32),
        in_specs=[any_spec, any_spec, pl.BlockSpec(memory_space=pltpu.VMEM), any_spec, any_spec, any_spec],
        out_specs=any_spec,
        scratch_shapes=[
            pltpu.VMEM((CHUNKS, 2, STEPS, KDEV, LANES), bf16),
            pltpu.VMEM((2, KDEV, STEPS, NO * NO), bf16),
            pltpu.VMEM((3, 256, 256), bf16),
            pltpu.VMEM((512, 256), bf16),
            pltpu.SMEM((HIST,), jnp.int32),
            pltpu.VMEM((8, LANES), f32),
            pltpu.VMEM((MOM, 8, LANES), f32),
            pltpu.VMEM((HIST, GROUPS, 8, LANES), f32),
            blocks, blocks, blocks, blocks,
            pltpu.VMEM((KDEV * STEPS, LANES), f32),
            pltpu.VMEM((GROUPS, 2, NO * NO, LANES), f32),
            pltpu.VMEM((GROUPS, 2, LANES, LANES), f32),
            pltpu.VMEM((GROUPS, 2, LANES, LANES), f32),
            parts, parts,
            pltpu.VMEM((CHUNKS, 2, KDEV, LANES), f32),
            dma((CHUNKS,)), dma((4,)), dma, dma,
            dma((CHUNKS,)), dma((CHUNKS,)), dma((CHUNKS,)), dma((CHUNKS,)), dma((CHUNKS,)), dma((CHUNKS,)), dma((CHUNKS,)),
        ],
        compiler_params=pltpu.CompilerParams(collective_id=0, has_side_effects=True, vmem_limit_bytes=48 << 20),
    )(greens, advanced, coupling, bounds, jnp.asarray(tabs), jnp.asarray(space_tab))


def solution(mesh):
    in_specs = (P(None, "hist", "mom", None), P(None, "mom", "hist", None), P("mom"), P())
    out_specs = P("hist", None, "mom", None)
    return jax.shard_map(per_device, mesh=mesh, in_specs=in_specs, out_specs=out_specs, check_vma=False)
```

```python
import functools
import math

import jax
import jax.numpy as jnp
import ml_dtypes
import numpy as np
from jax import lax
from jax.experimental import pallas as pl
from jax.experimental.pallas import tpu as pltpu
from jax.sharding import PartitionSpec as P

MESH = pl.DeviceIdType.MESH
L = 32
NO = 32
LANES = 128
CHUNKS = 8
MOM = 16
HIST = 8
STEPS = 8
KDEV = 64
AHEAD = 3
BACK = 2
LAST = 2


def tables():
    index = np.arange(L, dtype=np.int32)
    phase = index[:, None] * index[None, :] % L
    angle = phase.astype(np.float32) * np.float32(2.0 * math.pi / L)
    norm = np.float32(1.0 / math.sqrt(L))
    cosines = (np.cos(angle) * norm).astype(ml_dtypes.bfloat16).astype(np.float32)
    sines = (np.sin(angle) * norm).astype(ml_dtypes.bfloat16).astype(np.float32)
    ahead = np.array([[cosines, -sines], [sines, cosines]])
    back = np.array([[cosines, sines], [-sines, cosines]])
    eye = np.eye(2, dtype=np.float32)
    group = np.array([[0, 16]] + [[m, L - m] for m in range(1, MOM)])
    flip = (-index) % L
    pairs = np.arange(L).reshape(MOM, 2)

    first = np.einsum("ridyk,st,lm->dsyrlitmk", ahead[:, :, group, :].reshape(2, 2, MOM, 2, L), eye, eye)
    along = ahead[:, :, :, pairs]
    space = np.einsum("rixdl,st,yw->rsyxdtwil", along, eye, eye)
    turned = along[:, :, flip]
    mirror = np.einsum("rixdl,st,yw->rsyxdtwil", turned, eye, eye[::-1])
    mirror_own = np.einsum("rixdl,st,yw->rsyxdtwil", turned, eye, eye)
    third = np.einsum("ridlx,st,yw->dlsyritwx", back[:, :, pairs, :], eye, eye)
    last = np.einsum("rikdy,st->rskdtyi", back[:, :, :, group], np.eye(4, dtype=np.float32))
    square = lambda a: a.reshape(256, 256)
    moved = [np.concatenate([square(space), square(m)]) for m in (mirror, mirror_own)]
    return (
        np.stack([square(first), square(third), square(last)]).astype(ml_dtypes.bfloat16),
        np.stack(moved).astype(ml_dtypes.bfloat16),
    )


def other(me, d):
    return lax.rem(me // 4 + d // 4, 4) * 4 + lax.rem(lax.rem(me, 4) + d % 4, 4)


def kernel(
    greens, advanced, coupling, bounds, tabs, space_tab, out,
    gbuf, abuf, tbuf, sbuf, bbuf, cbuf, own_c, all_c, masks,
    s1, r1, s2, r2, rows, bt, at, acc, cs, cr,
    in_sem, load_sem, c_send, c_recv, s1_send, r1_recv, s2_send, r2_recv, cs_send, cr_recv,
):
    me = lax.axis_index("mom")
    h = lax.axis_index("hist")

    def lanes(c):
        return pl.ds(pl.multiple_of(c * LANES, LANES), LANES)

    pick = jnp.where(me == 0, 1, 0)
    tab_copy = pltpu.make_async_copy(tabs, tbuf, load_sem.at[0])
    space_copy = pltpu.make_async_copy(space_tab.at[pick], sbuf, load_sem.at[1])
    adv_copy = pltpu.make_async_copy(advanced, abuf, load_sem.at[2])
    bound_copy = pltpu.make_async_copy(bounds, bbuf, load_sem.at[3])

    def green_copy(c):
        return pltpu.make_async_copy(greens.at[:, :, :, lanes(c)], gbuf.at[c], in_sem.at[c])

    coupling_load = pltpu.make_async_copy(coupling, cbuf, load_sem.at[4])
    coupling_load.start()
    tab_copy.start()
    green_copy(0).start()
    green_copy(1).start()
    space_copy.start()
    bound_copy.start()

    barrier = pltpu.get_barrier_semaphore()
    for d in range(1, MOM):
        pl.semaphore_signal(barrier, inc=1, device_id=(other(me, d), h), device_id_type=MESH)
    for d in range(1, HIST):
        pl.semaphore_signal(barrier, inc=1, device_id=(me, lax.rem(h + d, HIST)), device_id_type=MESH)

    for c in range(2, CHUNKS):
        green_copy(c).start()
    adv_copy.start()

    def exchange(src, dst, send, recv, c):
        for d in range(1, MOM):
            p = other(me, d)
            pltpu.make_async_remote_copy(
                src_ref=src.at[c, p], dst_ref=dst.at[c, me], send_sem=send.at[c], recv_sem=recv.at[c],
                device_id=(p, h), device_id_type=MESH,
            ).start()
        dst[c, me] = src[c, me]

    def arrivals(src, dst, send, recv, c):
        return pltpu.make_async_remote_copy(
            src_ref=src.at[c, pl.ds(0, MOM - 1)], dst_ref=dst.at[c, pl.ds(0, MOM - 1)],
            send_sem=send.at[c], recv_sem=recv.at[c], device_id=(other(me, 1), h), device_id_type=MESH,
        )

    def coupling_copy(p):
        return pltpu.make_async_remote_copy(
            src_ref=own_c, dst_ref=all_c.at[me], send_sem=c_send, recv_sem=c_recv,
            device_id=(p, h), device_id_type=MESH,
        )

    def coupling_all():
        return pltpu.make_async_remote_copy(
            src_ref=all_c.at[pl.ds(0, MOM - 1)], dst_ref=all_c.at[pl.ds(0, MOM - 1)], send_sem=c_send, recv_sem=c_recv,
            device_id=(other(me, 1), h), device_id_type=MESH,
        )

    def partial_all(c, low):
        return pltpu.make_async_remote_copy(
            src_ref=cs.at[c, low, pl.ds(0, HIST - 1)], dst_ref=cr.at[c, low, pl.ds(0, HIST - 1)],
            send_sem=cs_send.at[c, low], recv_sem=cr_recv.at[c, low], device_id=(me, lax.rem(h + 1, HIST)), device_id_type=MESH,
        )

    def two(load, q):
        return jnp.concatenate([load(2 * q), load(2 * q + 1)], axis=1)

    def spread(dst, c, q, value):
        value = value.astype(jnp.bfloat16)
        for n in range(2):
            part = value[:, n * LANES:(n + 1) * LANES].reshape(MOM, 16, LANES)
            dst[c, :, pl.ds((2 * q + n) * 16, 16), :] = part

    def gathered(src, c, first=0):
        return lambda g: src[c, :, pl.ds(first + g * 16, 16), :].reshape(256, LANES)

    def forward(c):
        green_copy(c).wait()
        for q in range(2):
            data = two(lambda g: gbuf[c, :, pl.ds(2 * g, 2)].reshape(256, LANES), q)
            spread(s1, c, q, jnp.dot(tbuf[0], data, preferred_element_type=jnp.float32))

    def middle(c):
        arrivals(s1, r1, s1_send, r1_recv, c).wait_recv()
        low = lax.broadcasted_iota(jnp.int32, (1, LANES), 1) < LANES // 2
        weight = jnp.where(low, all_c[2 * c, 0:1, :], all_c[2 * c + 1, 0:1, :])
        weight = weight * weight
        weight = jnp.concatenate([weight, weight], axis=1)
        for q in range(2):
            data = two(gathered(r1, c), q)
            space = jnp.dot(sbuf[...], data, preferred_element_type=jnp.float32)
            re, im, mre, mim = (space[n * 128:(n + 1) * 128] for n in range(4))
            square_re = re * re - im * im
            square_im = 2.0 * re * im
            sigma_re = weight * (square_re * mre + square_im * mim)
            sigma_im = weight * (square_im * mre - square_re * mim)
            sigma = jnp.concatenate([sigma_re.astype(jnp.bfloat16), sigma_im.astype(jnp.bfloat16)], axis=0)
            value = jnp.dot(tbuf[1], sigma, preferred_element_type=jnp.float32).reshape(MOM, 2, 8, 2 * LANES)
            value = jnp.concatenate([value[..., :LANES], value[..., LANES:]], axis=2).astype(jnp.bfloat16)
            for low in range(2):
                s2[c, :, pl.ds(low * 32 + q * 16, 16), :] = value[:, low]

    def products(c, low):
        final = jnp.dot(tbuf[2], two(gathered(r2, c, low * 32), 0), preferred_element_type=jnp.float32)
        for g in range(2):
            re = final[:128, g * LANES:(g + 1) * LANES].T
            im = final[128:, g * LANES:(g + 1) * LANES].T
            at[g, 0] = re
            at[g, 1] = im
            at[g, 2] = re + im

        def one_block(n, carry):
            g, first = n // 2, lax.rem(n, 2) * (2 * NO)

            def one_orbital(m, sums):
                b = [bt[low, g, part, pl.ds(pl.multiple_of(m * NO, NO), NO), :] for part in range(3)]
                result = []
                for a in range(2):
                    for part in range(3):
                        factor = at[g, part, pl.ds(first + a * NO + m, 1), :]
                        result.append(sums[3 * a + part] + factor * b[part])
                return tuple(result)

            zero = jnp.zeros((NO, LANES), jnp.float32)
            sums = lax.fori_loop(0, NO, one_orbital, (zero,) * 6, unroll=8)
            for a in range(2):
                re_re, im_im, both = sums[3 * a:3 * a + 3]
                spot = pl.ds(pl.multiple_of(first + a * NO, NO), NO)
                acc[g, 0, spot, :] = (re_re - im_im).astype(jnp.bfloat16)
                acc[g, 1, spot, :] = (both - (re_re + im_im)).astype(jnp.bfloat16)
            return carry

        lax.fori_loop(0, 4, one_block, 0)
        terms = jnp.concatenate([acc[g].reshape(2 * LANES, LANES) for g in range(2)], axis=1)
        sums = lax.dot_general(masks[...], terms, (((1,), (1,)), ((), ())), preferred_element_type=jnp.float32)
        cs[c, low] = sums.astype(jnp.bfloat16).reshape(HIST, 32, 2 * LANES)
        for d in range(1, HIST):
            p = lax.rem(h + d, HIST)
            pltpu.make_async_remote_copy(
                src_ref=cs.at[c, low, p], dst_ref=cr.at[c, low, h],
                send_sem=cs_send.at[c, low], recv_sem=cr_recv.at[c, low],
                device_id=(me, p), device_id_type=MESH,
            ).start()

    def finish(c):
        for low in range(2):
            partial_all(c, low).wait_recv()
            total = cs[c, low, h].astype(jnp.float32)
            for d in range(1, HIST):
                total = total + cr[c, low, lax.rem(h + d, HIST)].astype(jnp.float32)
            for part in range(2):
                out[0, part, pl.ds(low * 32, 32), lanes(c)] = total[:, part * LANES:(part + 1) * LANES]

    def prepare_masks():
        bound_copy.wait()
        row_ky = lax.broadcasted_iota(jnp.int32, (32, 256), 0)
        column = lax.broadcasted_iota(jnp.int32, (32, 256), 1)
        step = h * STEPS + column // 32
        for j in range(HIST):
            keep = (step < bbuf[j]) & (column % 32 == row_ky)
            masks[pl.ds(32 * j, 32), :] = jnp.where(keep, 1.0 / math.sqrt(STEPS * HIST), 0.0).astype(jnp.bfloat16)

    def prepare_advanced():
        adv_copy.wait()

        def one(t, carry):
            for part in range(2):
                rows[part] = abuf[part, :, :, lanes(t)].astype(jnp.float32).reshape(KDEV * STEPS, LANES)
            spot = pl.ds(pl.multiple_of(t * LANES, LANES), LANES)
            for low in range(2):
                for g in range(2):
                    pair = []
                    for part in range(2):
                        pieces = [rows[part, pl.ds(low * 256 + 4 * g + s, 32, STEPS), :] for s in range(4)]
                        pair.append(jnp.concatenate(pieces, axis=0).T)
                        bt[low, g, part, spot, :] = pair[part]
                    bt[low, g, 2, spot, :] = pair[0] + pair[1]
            return carry

        lax.fori_loop(0, CHUNKS, one, 0)

    coupling_load.wait()
    pair = cbuf[...].reshape(1, KDEV)
    own_c[...] = jnp.broadcast_to(jnp.concatenate([pair, pair], axis=1), (8, LANES))
    all_c[me] = own_c[...]
    tab_copy.wait()
    forward(0)
    pl.semaphore_wait(barrier, MOM - 1 + HIST - 1)
    for d in range(1, MOM):
        coupling_copy(other(me, d)).start()
    exchange(s1, r1, s1_send, r1_recv, 0)

    def send_ahead(c, carry):
        forward(c)
        exchange(s1, r1, s1_send, r1_recv, c)
        return carry

    lax.fori_loop(1, AHEAD, send_ahead, 0)
    prepare_masks()
    prepare_advanced()
    space_copy.wait()
    coupling_all().wait_recv()

    def step(i, carry):
        @pl.when(i < CHUNKS)
        def _():
            middle(i)
            exchange(s2, r2, s2_send, r2_recv, i)

        @pl.when(i + AHEAD < CHUNKS)
        def _():
            send_ahead(i + AHEAD, 0)

        @pl.when((i >= BACK) & (i < CHUNKS + BACK))
        def _():
            arrivals(s2, r2, s2_send, r2_recv, i - BACK).wait_recv()
            for low in range(2):
                products(i - BACK, low)

        @pl.when(i >= BACK + LAST)
        def _():
            finish(i - BACK - LAST)

        return carry

    lax.fori_loop(0, CHUNKS + BACK + LAST, step, 0)

    def drain(c, carry):
        arrivals(s1, r1, s1_send, r1_recv, c).wait_send()
        arrivals(s2, r2, s2_send, r2_recv, c).wait_send()
        for low in range(2):
            partial_all(c, low).wait_send()
        return carry

    coupling_all().wait_send()
    lax.fori_loop(0, CHUNKS, drain, 0)


def per_device(greens, advanced, coupling, bounds):
    tabs, space_tab = tables()
    any_spec = pl.BlockSpec(memory_space=pltpu.HBM)
    bf16, f32 = jnp.bfloat16, jnp.float32
    dma = pltpu.SemaphoreType.DMA
    blocks = pltpu.VMEM((CHUNKS, MOM, 64, LANES), bf16)
    parts = pltpu.VMEM((CHUNKS, 2, HIST, 32, 2 * LANES), bf16)
    return pl.pallas_call(
        kernel,
        out_shape=pltpu.VMEM((1, 2, KDEV, NO * NO), f32),
        in_specs=[any_spec] * 6,
        out_specs=pl.BlockSpec(memory_space=pltpu.VMEM),
        scratch_shapes=[
            pltpu.VMEM((CHUNKS, 2, STEPS, KDEV, LANES), bf16),
            pltpu.VMEM((2, KDEV, STEPS, NO * NO), bf16),
            pltpu.VMEM((3, 256, 256), bf16),
            pltpu.VMEM((512, 256), bf16),
            pltpu.SMEM((HIST,), jnp.int32),
            pltpu.VMEM((KDEV,), f32),
            pltpu.VMEM((8, LANES), f32),
            pltpu.VMEM((MOM, 8, LANES), f32),
            pltpu.VMEM((256, 256), bf16),
            blocks, blocks, blocks, blocks,
            pltpu.VMEM((2, KDEV * STEPS, LANES), f32),
            pltpu.VMEM((2, 2, 3, NO * NO, LANES), f32),
            pltpu.VMEM((2, 3, LANES, LANES), f32),
            pltpu.VMEM((2, 2, LANES, LANES), bf16),
            parts, parts,
            dma((CHUNKS,)), dma((5,)), dma, dma,
            dma((CHUNKS,)), dma((CHUNKS,)), dma((CHUNKS,)), dma((CHUNKS,)), dma((CHUNKS, 2)), dma((CHUNKS, 2)),
        ],
        compiler_params=pltpu.CompilerParams(collective_id=0, has_side_effects=True, vmem_limit_bytes=63 << 20),
    )(greens, advanced, coupling, bounds, jnp.asarray(tabs), jnp.asarray(space_tab))


def solution(mesh):
    in_specs = (P(None, "hist", "mom", None), P(None, "mom", "hist", None), P("mom"), P())
    out_specs = P("hist", None, "mom", None)
    return jax.shard_map(per_device, mesh=mesh, in_specs=in_specs, out_specs=out_specs, check_vma=False)
```

```python
import functools
import math

import jax
import jax.numpy as jnp
import ml_dtypes
import numpy as np
from jax import lax
from jax.experimental import pallas as pl
from jax.experimental.pallas import tpu as pltpu
from jax.sharding import PartitionSpec as P

MESH = pl.DeviceIdType.MESH
L = 32
NO = 32
LANES = 128
CHUNKS = 8
MOM = 16
HIST = 8
STEPS = 8
KDEV = 64
AHEAD = 3
BACK = 2
LAST = 2


def tables():
    index = np.arange(L, dtype=np.int32)
    phase = index[:, None] * index[None, :] % L
    angle = phase.astype(np.float32) * np.float32(2.0 * math.pi / L)
    norm = np.float32(1.0 / math.sqrt(L))
    cosines = (np.cos(angle) * norm).astype(ml_dtypes.bfloat16).astype(np.float32)
    sines = (np.sin(angle) * norm).astype(ml_dtypes.bfloat16).astype(np.float32)
    ahead = np.array([[cosines, -sines], [sines, cosines]])
    back = np.array([[cosines, sines], [-sines, cosines]])
    eye = np.eye(2, dtype=np.float32)
    group = np.array([[0, 16]] + [[m, L - m] for m in range(1, MOM)])
    flip = (-index) % L
    pairs = np.arange(L).reshape(MOM, 2)

    first = np.einsum("ridyk,st,lm->dsyrlitmk", ahead[:, :, group, :].reshape(2, 2, MOM, 2, L), eye, eye)
    along = ahead[:, :, :, pairs]
    space = np.einsum("rixdl,st,yw->rsyxdtwil", along, eye, eye)
    turned = along[:, :, flip]
    mirror = np.einsum("rixdl,st,yw->rsyxdtwil", turned, eye, eye[::-1])
    mirror_own = np.einsum("rixdl,st,yw->rsyxdtwil", turned, eye, eye)
    third = np.einsum("ridlx,st,yw->dlsyritwx", back[:, :, pairs, :], eye, eye)
    last = np.einsum("rikdy,st->rskdtyi", back[:, :, :, group], np.eye(4, dtype=np.float32))
    square = lambda a: a.reshape(256, 256)
    moved = [np.concatenate([square(space), square(m)]) for m in (mirror, mirror_own)]
    return (
        np.stack([square(first), square(third), square(last)]).astype(ml_dtypes.bfloat16),
        np.stack(moved).astype(ml_dtypes.bfloat16),
    )


def other(me, d):
    return lax.rem(me // 4 + d // 4, 4) * 4 + lax.rem(lax.rem(me, 4) + d % 4, 4)


def kernel(
    greens, advanced, coupling, bounds, tabs, space_tab, out,
    gbuf, abuf, tbuf, sbuf, bbuf, cbuf, own_c, all_c, masks,
    s1, r1, s2, r2, rows, bt, at, acc, cs, cr,
    in_sem, load_sem, c_send, c_recv, s1_send, r1_recv, s2_send, r2_recv, cs_send, cr_recv,
):
    me = lax.axis_index("mom")
    h = lax.axis_index("hist")

    def lanes(c):
        return pl.ds(pl.multiple_of(c * LANES, LANES), LANES)

    pick = jnp.where(me == 0, 1, 0)
    tab_copy = pltpu.make_async_copy(tabs, tbuf, load_sem.at[0])
    space_copy = pltpu.make_async_copy(space_tab.at[pick], sbuf, load_sem.at[1])
    adv_copy = pltpu.make_async_copy(advanced, abuf, load_sem.at[2])
    bound_copy = pltpu.make_async_copy(bounds, bbuf, load_sem.at[3])

    def green_copy(c):
        return pltpu.make_async_copy(greens.at[:, :, :, lanes(c)], gbuf.at[c], in_sem.at[c])

    barrier = pltpu.get_barrier_semaphore()
    for d in range(1, MOM):
        pl.semaphore_signal(barrier, inc=1, device_id=(other(me, d), h), device_id_type=MESH)
    for d in range(1, HIST):
        pl.semaphore_signal(barrier, inc=1, device_id=(me, lax.rem(h + d, HIST)), device_id_type=MESH)

    coupling_load = pltpu.make_async_copy(coupling, cbuf, load_sem.at[4])
    coupling_load.start()
    tab_copy.start()
    green_copy(0).start()
    green_copy(1).start()
    space_copy.start()
    bound_copy.start()

    for c in range(2, CHUNKS):
        green_copy(c).start()
    adv_copy.start()

    def exchange(src, dst, send, recv, c):
        for d in range(1, MOM):
            p = other(me, d)
            pltpu.make_async_remote_copy(
                src_ref=src.at[c, p], dst_ref=dst.at[c, me], send_sem=send.at[c], recv_sem=recv.at[c],
                device_id=(p, h), device_id_type=MESH,
            ).start()
        dst[c, me] = src[c, me]

    def exchange_back(c):
        for low in range(2):
            half = pl.ds(low * 32, 32)
            for d in range(1, MOM):
                p = other(me, d)
                pltpu.make_async_remote_copy(
                    src_ref=s2.at[c, p, half], dst_ref=r2.at[c, me, half],
                    send_sem=s2_send.at[c], recv_sem=r2_recv.at[c, low],
                    device_id=(p, h), device_id_type=MESH,
                ).start()
        r2[c, me] = s2[c, me]

    def arrivals_back(c, low):
        half = pl.ds(low * 32, 32)
        return pltpu.make_async_remote_copy(
            src_ref=s2.at[c, pl.ds(0, MOM - 1), half], dst_ref=r2.at[c, pl.ds(0, MOM - 1), half],
            send_sem=s2_send.at[c], recv_sem=r2_recv.at[c, low], device_id=(other(me, 1), h), device_id_type=MESH,
        )

    def arrivals(src, dst, send, recv, c):
        return pltpu.make_async_remote_copy(
            src_ref=src.at[c, pl.ds(0, MOM - 1)], dst_ref=dst.at[c, pl.ds(0, MOM - 1)],
            send_sem=send.at[c], recv_sem=recv.at[c], device_id=(other(me, 1), h), device_id_type=MESH,
        )

    def coupling_copy(p):
        return pltpu.make_async_remote_copy(
            src_ref=own_c, dst_ref=all_c.at[me], send_sem=c_send, recv_sem=c_recv,
            device_id=(p, h), device_id_type=MESH,
        )

    def coupling_all():
        return pltpu.make_async_remote_copy(
            src_ref=all_c.at[pl.ds(0, MOM - 1)], dst_ref=all_c.at[pl.ds(0, MOM - 1)], send_sem=c_send, recv_sem=c_recv,
            device_id=(other(me, 1), h), device_id_type=MESH,
        )

    def partial_all(c, low):
        return pltpu.make_async_remote_copy(
            src_ref=cs.at[c, low, pl.ds(0, HIST - 1)], dst_ref=cr.at[c, low, pl.ds(0, HIST - 1)],
            send_sem=cs_send.at[c, low], recv_sem=cr_recv.at[c, low], device_id=(me, lax.rem(h + 1, HIST)), device_id_type=MESH,
        )

    def two(load, q):
        return jnp.concatenate([load(2 * q), load(2 * q + 1)], axis=1)

    def spread(dst, c, q, value):
        value = value.astype(jnp.bfloat16)
        for n in range(2):
            part = value[:, n * LANES:(n + 1) * LANES].reshape(MOM, 16, LANES)
            dst[c, :, pl.ds((2 * q + n) * 16, 16), :] = part

    def gathered(src, c, first=0):
        return lambda g: src[c, :, pl.ds(first + g * 16, 16), :].reshape(256, LANES)

    def forward(c):
        green_copy(c).wait()
        for q in range(2):
            data = two(lambda g: gbuf[c, :, pl.ds(2 * g, 2)].reshape(256, LANES), q)
            spread(s1, c, q, jnp.dot(tbuf[0], data, preferred_element_type=jnp.float32))

    def middle(c):
        arrivals(s1, r1, s1_send, r1_recv, c).wait_recv()
        low = lax.broadcasted_iota(jnp.int32, (1, LANES), 1) < LANES // 2
        weight = jnp.where(low, all_c[2 * c, 0:1, :], all_c[2 * c + 1, 0:1, :])
        weight = weight * weight
        weight = jnp.concatenate([weight, weight], axis=1)
        for q in range(2):
            data = two(gathered(r1, c), q)
            space = jnp.dot(sbuf[...], data, preferred_element_type=jnp.float32)
            re, im, mre, mim = (space[n * 128:(n + 1) * 128] for n in range(4))
            square_re = re * re - im * im
            square_im = 2.0 * re * im
            sigma_re = weight * (square_re * mre + square_im * mim)
            sigma_im = weight * (square_im * mre - square_re * mim)
            sigma = jnp.concatenate([sigma_re.astype(jnp.bfloat16), sigma_im.astype(jnp.bfloat16)], axis=0)
            value = jnp.dot(tbuf[1], sigma, preferred_element_type=jnp.float32).reshape(MOM, 2, 8, 2 * LANES)
            value = jnp.concatenate([value[..., :LANES], value[..., LANES:]], axis=2).astype(jnp.bfloat16)
            for low in range(2):
                s2[c, :, pl.ds(low * 32 + q * 16, 16), :] = value[:, low]

    def products(c, low):
        final = jnp.dot(tbuf[2], two(gathered(r2, c, low * 32), 0), preferred_element_type=jnp.float32)
        for g in range(2):
            re = final[:128, g * LANES:(g + 1) * LANES].T
            im = final[128:, g * LANES:(g + 1) * LANES].T
            at[g, 0] = re
            at[g, 1] = im
            at[g, 2] = re + im

        def one_block(n, carry):
            g, first = n // 2, n % 2 * (2 * NO)

            def one_orbital(m, sums):
                b = [bt[low, g, part, pl.ds(pl.multiple_of(m * NO, NO), NO), :] for part in range(3)]
                result = []
                for a in range(2):
                    for part in range(3):
                        factor = at[g, part, pl.ds(first + a * NO + m, 1), :]
                        result.append(sums[3 * a + part] + factor * b[part])
                return tuple(result)

            zero = jnp.zeros((NO, LANES), jnp.float32)
            sums = lax.fori_loop(0, NO, one_orbital, (zero,) * 6, unroll=32)
            for a in range(2):
                re_re, im_im, both = sums[3 * a:3 * a + 3]
                spot = pl.ds(first + a * NO, NO)
                acc[g, 0, spot, :] = (re_re - im_im).astype(jnp.bfloat16)
                acc[g, 1, spot, :] = (both - (re_re + im_im)).astype(jnp.bfloat16)
            return carry

        for n in range(4):
            one_block(n, 0)
        terms = jnp.concatenate([acc[g].reshape(2 * LANES, LANES) for g in range(2)], axis=1)
        sums = lax.dot_general(masks[...], terms, (((1,), (1,)), ((), ())), preferred_element_type=jnp.float32)
        cs[c, low] = sums.astype(jnp.bfloat16).reshape(HIST, 32, 2 * LANES)
        for d in (4, 5, 3, 2, 6, 7, 1):
            p = lax.rem(h + d, HIST)
            pltpu.make_async_remote_copy(
                src_ref=cs.at[c, low, p], dst_ref=cr.at[c, low, h],
                send_sem=cs_send.at[c, low], recv_sem=cr_recv.at[c, low],
                device_id=(me, p), device_id_type=MESH,
            ).start()

    def finish(c):
        for low in range(2):
            partial_all(c, low).wait_recv()
            total = cs[c, low, h].astype(jnp.float32)
            for d in range(1, HIST):
                total = total + cr[c, low, lax.rem(h + d, HIST)].astype(jnp.float32)
            for part in range(2):
                out[0, part, pl.ds(low * 32, 32), lanes(c)] = total[:, part * LANES:(part + 1) * LANES]

    def prepare_masks():
        bound_copy.wait()
        row_ky = lax.broadcasted_iota(jnp.int32, (32, 256), 0)
        column = lax.broadcasted_iota(jnp.int32, (32, 256), 1)
        step = h * STEPS + column // 32
        for j in range(HIST):
            keep = (step < bbuf[j]) & (column % 32 == row_ky)
            masks[pl.ds(32 * j, 32), :] = jnp.where(keep, 1.0 / math.sqrt(STEPS * HIST), 0.0).astype(jnp.bfloat16)

    def prepare_advanced():
        adv_copy.wait()

        def one(t, carry):
            for part in range(2):
                rows[part] = abuf[part, :, :, lanes(t)].astype(jnp.float32).reshape(KDEV * STEPS, LANES)
            spot = pl.ds(pl.multiple_of(t * LANES, LANES), LANES)
            for low in range(2):
                for g in range(2):
                    pair = []
                    for part in range(2):
                        pieces = [rows[part, pl.ds(low * 256 + 4 * g + s, 32, STEPS), :] for s in range(4)]
                        pair.append(jnp.concatenate(pieces, axis=0).T)
                        bt[low, g, part, spot, :] = pair[part]
                    bt[low, g, 2, spot, :] = pair[0] + pair[1]
            return carry

        lax.fori_loop(0, CHUNKS, one, 0)

    coupling_load.wait()
    pair = cbuf[...].reshape(1, KDEV)
    own_c[...] = jnp.broadcast_to(jnp.concatenate([pair, pair], axis=1), (8, LANES))
    all_c[me] = own_c[...]
    tab_copy.wait()
    forward(0)
    pl.semaphore_wait(barrier, MOM - 1 + HIST - 1)
    exchange(s1, r1, s1_send, r1_recv, 0)
    for d in range(1, MOM):
        coupling_copy(other(me, d)).start()

    def send_ahead(c, carry):
        forward(c)
        exchange(s1, r1, s1_send, r1_recv, c)
        return carry

    lax.fori_loop(1, AHEAD, send_ahead, 0)
    prepare_masks()
    prepare_advanced()
    space_copy.wait()
    coupling_all().wait_recv()

    def step(i, carry):
        @pl.when(i < CHUNKS)
        def _():
            middle(i)
            exchange_back(i)

        @pl.when(i + AHEAD < CHUNKS)
        def _():
            send_ahead(i + AHEAD, 0)

        @pl.when((i >= BACK) & (i < CHUNKS + BACK))
        def _():
            for low in range(2):
                arrivals_back(i - BACK, low).wait_recv()
                products(i - BACK, low)

        @pl.when(i >= BACK + LAST)
        def _():
            finish(i - BACK - LAST)

        return carry

    lax.fori_loop(0, CHUNKS + BACK + LAST, step, 0)

    def drain(c, carry):
        arrivals(s1, r1, s1_send, r1_recv, c).wait_send()
        for low in range(2):
            arrivals_back(c, low).wait_send()
        for low in range(2):
            partial_all(c, low).wait_send()
        return carry

    coupling_all().wait_send()
    lax.fori_loop(0, CHUNKS, drain, 0)


def per_device(greens, advanced, coupling, bounds):
    tabs, space_tab = tables()
    any_spec = pl.BlockSpec(memory_space=pltpu.HBM)
    bf16, f32 = jnp.bfloat16, jnp.float32
    dma = pltpu.SemaphoreType.DMA
    blocks = pltpu.VMEM((CHUNKS, MOM, 64, LANES), bf16)
    parts = pltpu.VMEM((CHUNKS, 2, HIST, 32, 2 * LANES), bf16)
    return pl.pallas_call(
        kernel,
        out_shape=pltpu.VMEM((1, 2, KDEV, NO * NO), f32),
        in_specs=[any_spec] * 6,
        out_specs=pl.BlockSpec(memory_space=pltpu.VMEM),
        scratch_shapes=[
            pltpu.VMEM((CHUNKS, 2, STEPS, KDEV, LANES), bf16),
            pltpu.VMEM((2, KDEV, STEPS, NO * NO), bf16),
            pltpu.VMEM((3, 256, 256), bf16),
            pltpu.VMEM((512, 256), bf16),
            pltpu.SMEM((HIST,), jnp.int32),
            pltpu.VMEM((KDEV,), f32),
            pltpu.VMEM((8, LANES), f32),
            pltpu.VMEM((MOM, 8, LANES), f32),
            pltpu.VMEM((256, 256), bf16),
            blocks, blocks, blocks, blocks,
            pltpu.VMEM((2, KDEV * STEPS, LANES), f32),
            pltpu.VMEM((2, 2, 3, NO * NO, LANES), f32),
            pltpu.VMEM((2, 3, LANES, LANES), f32),
            pltpu.VMEM((2, 2, LANES, LANES), bf16),
            parts, parts,
            dma((CHUNKS,)), dma((5,)), dma, dma,
            dma((CHUNKS,)), dma((CHUNKS,)), dma((CHUNKS,)), dma((CHUNKS, 2)), dma((CHUNKS, 2)), dma((CHUNKS, 2)),
        ],
        compiler_params=pltpu.CompilerParams(collective_id=0, has_side_effects=True, vmem_limit_bytes=63 << 20),
    )(greens, advanced, coupling, bounds, jnp.asarray(tabs), jnp.asarray(space_tab))


def solution(mesh):
    in_specs = (P(None, "hist", "mom", None), P(None, "mom", "hist", None), P("mom"), P())
    out_specs = P("hist", None, "mom", None)
    return jax.shard_map(per_device, mesh=mesh, in_specs=in_specs, out_specs=out_specs, check_vma=False)
```

```python
import functools
import math

import jax
import jax.numpy as jnp
import ml_dtypes
import numpy as np
from jax import lax
from jax.experimental import pallas as pl
from jax.experimental.pallas import tpu as pltpu
from jax.sharding import PartitionSpec as P

MESH = pl.DeviceIdType.MESH
L = 32
NO = 32
LANES = 128
CHUNKS = 8
MOM = 16
HIST = 8
STEPS = 8
KDEV = 64
AHEAD = 4
BACK = 3
LAST = 2


def tables():
    index = np.arange(L, dtype=np.int32)
    phase = index[:, None] * index[None, :] % L
    angle = phase.astype(np.float32) * np.float32(2.0 * math.pi / L)
    norm = np.float32(1.0 / math.sqrt(L))
    cosines = (np.cos(angle) * norm).astype(ml_dtypes.bfloat16).astype(np.float32)
    sines = (np.sin(angle) * norm).astype(ml_dtypes.bfloat16).astype(np.float32)
    ahead = np.array([[cosines, -sines], [sines, cosines]])
    back = np.array([[cosines, sines], [-sines, cosines]])
    eye = np.eye(2, dtype=np.float32)
    group = np.array([[0, 16]] + [[m, L - m] for m in range(1, MOM)])
    flip = (-index) % L
    pairs = np.arange(L).reshape(MOM, 2)

    first = np.einsum("ridyk,st,lm->dsyrlitmk", ahead[:, :, group, :].reshape(2, 2, MOM, 2, L), eye, eye)
    along = ahead[:, :, :, pairs]
    space = np.einsum("rixdl,st,yw->rsyxdtwil", along, eye, eye)
    turned = along[:, :, flip]
    mirror = np.einsum("rixdl,st,yw->rsyxdtwil", turned, eye, eye[::-1])
    mirror_own = np.einsum("rixdl,st,yw->rsyxdtwil", turned, eye, eye)
    third = np.einsum("ridlx,st,yw->dlsyritwx", back[:, :, pairs, :], eye, eye)
    last = np.einsum("rikdy,st->rskdtyi", back[:, :, :, group], np.eye(4, dtype=np.float32))
    square = lambda a: a.reshape(256, 256)
    moved = [np.concatenate([square(space), square(m)]) for m in (mirror, mirror_own)]
    return (
        np.stack([square(first), square(third), square(last)]).astype(ml_dtypes.bfloat16),
        np.stack(moved).astype(ml_dtypes.bfloat16),
    )


def other(me, d):
    return lax.rem(me // 4 + d // 4, 4) * 4 + lax.rem(lax.rem(me, 4) + d % 4, 4)


def kernel(
    greens, advanced, coupling, bounds, tabs, space_tab, out,
    gbuf, abuf, tbuf, sbuf, bbuf, cbuf, own_c, all_c, masks,
    s1, r1, s2, r2, rows, bt, at, acc, cs, cr,
    in_sem, load_sem, c_send, c_recv, s1_send, r1_recv, s2_send, r2_recv, cs_send, cr_recv,
):
    me = lax.axis_index("mom")
    h = lax.axis_index("hist")

    def lanes(c):
        return pl.ds(pl.multiple_of(c * LANES, LANES), LANES)

    pick = jnp.where(me == 0, 1, 0)
    tab_copy = pltpu.make_async_copy(tabs, tbuf, load_sem.at[0])
    space_copy = pltpu.make_async_copy(space_tab.at[pick], sbuf, load_sem.at[1])
    adv_copy = pltpu.make_async_copy(advanced, abuf, load_sem.at[2])
    bound_copy = pltpu.make_async_copy(bounds, bbuf, load_sem.at[3])

    def green_copy(c):
        return pltpu.make_async_copy(greens.at[:, :, :, lanes(c)], gbuf.at[c], in_sem.at[c])

    barrier = pltpu.get_barrier_semaphore()
    for d in range(1, MOM):
        pl.semaphore_signal(barrier, inc=1, device_id=(other(me, d), h), device_id_type=MESH)
    for d in range(1, HIST):
        pl.semaphore_signal(barrier, inc=1, device_id=(me, lax.rem(h + d, HIST)), device_id_type=MESH)

    coupling_load = pltpu.make_async_copy(coupling, cbuf, load_sem.at[4])
    coupling_load.start()
    tab_copy.start()
    green_copy(0).start()
    green_copy(1).start()
    space_copy.start()
    bound_copy.start()

    for c in range(2, CHUNKS):
        green_copy(c).start()
    adv_copy.start()

    def exchange(src, dst, send, recv, c):
        for d in range(1, MOM):
            p = other(me, d)
            pltpu.make_async_remote_copy(
                src_ref=src.at[c, p], dst_ref=dst.at[c, me], send_sem=send.at[c], recv_sem=recv.at[c],
                device_id=(p, h), device_id_type=MESH,
            ).start()
        dst[c, me] = src[c, me]

    def exchange_back(c):
        for low in range(2):
            half = pl.ds(low * 32, 32)
            for d in range(1, MOM):
                p = other(me, d)
                pltpu.make_async_remote_copy(
                    src_ref=s2.at[c, p, half], dst_ref=r2.at[c, me, half],
                    send_sem=s2_send.at[c], recv_sem=r2_recv.at[c, low],
                    device_id=(p, h), device_id_type=MESH,
                ).start()
        r2[c, me] = s2[c, me]

    def arrivals_back(c, low):
        half = pl.ds(low * 32, 32)
        return pltpu.make_async_remote_copy(
            src_ref=s2.at[c, pl.ds(0, MOM - 1), half], dst_ref=r2.at[c, pl.ds(0, MOM - 1), half],
            send_sem=s2_send.at[c], recv_sem=r2_recv.at[c, low], device_id=(other(me, 1), h), device_id_type=MESH,
        )

    def arrivals(src, dst, send, recv, c):
        return pltpu.make_async_remote_copy(
            src_ref=src.at[c, pl.ds(0, MOM - 1)], dst_ref=dst.at[c, pl.ds(0, MOM - 1)],
            send_sem=send.at[c], recv_sem=recv.at[c], device_id=(other(me, 1), h), device_id_type=MESH,
        )

    def coupling_copy(p):
        return pltpu.make_async_remote_copy(
            src_ref=own_c, dst_ref=all_c.at[me], send_sem=c_send, recv_sem=c_recv,
            device_id=(p, h), device_id_type=MESH,
        )

    def coupling_all():
        return pltpu.make_async_remote_copy(
            src_ref=all_c.at[pl.ds(0, MOM - 1)], dst_ref=all_c.at[pl.ds(0, MOM - 1)], send_sem=c_send, recv_sem=c_recv,
            device_id=(other(me, 1), h), device_id_type=MESH,
        )

    def partial_all(c, low):
        return pltpu.make_async_remote_copy(
            src_ref=cs.at[c, low, pl.ds(0, HIST - 1)], dst_ref=cr.at[c, low, pl.ds(0, HIST - 1)],
            send_sem=cs_send.at[c, low], recv_sem=cr_recv.at[c, low], device_id=(me, lax.rem(h + 1, HIST)), device_id_type=MESH,
        )

    def two(load, q):
        return jnp.concatenate([load(2 * q), load(2 * q + 1)], axis=1)

    def spread(dst, c, q, value):
        value = value.astype(jnp.bfloat16)
        for n in range(2):
            part = value[:, n * LANES:(n + 1) * LANES].reshape(MOM, 16, LANES)
            dst[c, :, pl.ds((2 * q + n) * 16, 16), :] = part

    def gathered(src, c, first=0):
        return lambda g: src[c, :, pl.ds(first + g * 16, 16), :].reshape(256, LANES)

    def forward(c):
        green_copy(c).wait()
        for q in range(2):
            data = two(lambda g: gbuf[c, :, pl.ds(2 * g, 2)].reshape(256, LANES), q)
            spread(s1, c, q, jnp.dot(tbuf[0], data, preferred_element_type=jnp.float32))

    def middle(c):
        arrivals(s1, r1, s1_send, r1_recv, c).wait_recv()
        low = lax.broadcasted_iota(jnp.int32, (1, LANES), 1) < LANES // 2
        weight = jnp.where(low, all_c[2 * c, 0:1, :], all_c[2 * c + 1, 0:1, :])
        weight = weight * weight
        weight = jnp.concatenate([weight, weight], axis=1)
        for q in range(2):
            data = two(gathered(r1, c), q)
            space = jnp.dot(sbuf[...], data, preferred_element_type=jnp.float32)
            re, im, mre, mim = (space[n * 128:(n + 1) * 128] for n in range(4))
            square_re = re * re - im * im
            square_im = 2.0 * re * im
            sigma_re = weight * (square_re * mre + square_im * mim)
            sigma_im = weight * (square_im * mre - square_re * mim)
            sigma = jnp.concatenate([sigma_re.astype(jnp.bfloat16), sigma_im.astype(jnp.bfloat16)], axis=0)
            value = jnp.dot(tbuf[1], sigma, preferred_element_type=jnp.float32).reshape(MOM, 2, 8, 2 * LANES)
            value = jnp.concatenate([value[..., :LANES], value[..., LANES:]], axis=2).astype(jnp.bfloat16)
            for low in range(2):
                s2[c, :, pl.ds(low * 32 + q * 16, 16), :] = value[:, low]

    def products(c, low):
        final = jnp.dot(tbuf[2], two(gathered(r2, c, low * 32), 0), preferred_element_type=jnp.float32)
        for g in range(2):
            re = final[:128, g * LANES:(g + 1) * LANES].T
            im = final[128:, g * LANES:(g + 1) * LANES].T
            at[g, 0] = re
            at[g, 1] = im
            at[g, 2] = re + im

        def one_block(n, carry):
            g, first = n // 2, n % 2 * (2 * NO)

            def one_orbital(m, sums):
                b = [bt[low, g, part, pl.ds(pl.multiple_of(m * NO, NO), NO), :] for part in range(3)]
                result = []
                for a in range(2):
                    for part in range(3):
                        factor = at[g, part, pl.ds(first + a * NO + m, 1), :]
                        result.append(sums[3 * a + part] + factor * b[part])
                return tuple(result)

            zero = jnp.zeros((NO, LANES), jnp.float32)
            sums = lax.fori_loop(0, NO, one_orbital, (zero,) * 6, unroll=32)
            for a in range(2):
                re_re, im_im, both = sums[3 * a:3 * a + 3]
                spot = pl.ds(first + a * NO, NO)
                acc[g, 0, spot, :] = (re_re - im_im).astype(jnp.bfloat16)
                acc[g, 1, spot, :] = (both - (re_re + im_im)).astype(jnp.bfloat16)
            return carry

        for n in range(4):
            one_block(n, 0)
        terms = jnp.concatenate([acc[g].reshape(2 * LANES, LANES) for g in range(2)], axis=1)
        sums = lax.dot_general(masks[...], terms, (((1,), (1,)), ((), ())), preferred_element_type=jnp.float32)
        cs[c, low] = sums.astype(jnp.bfloat16).reshape(HIST, 32, 2 * LANES)
        for d in (4, 5, 3, 2, 6, 7, 1):
            p = lax.rem(h + d, HIST)
            pltpu.make_async_remote_copy(
                src_ref=cs.at[c, low, p], dst_ref=cr.at[c, low, h],
                send_sem=cs_send.at[c, low], recv_sem=cr_recv.at[c, low],
                device_id=(me, p), device_id_type=MESH,
            ).start()

    def finish(c):
        for low in range(2):
            partial_all(c, low).wait_recv()
            total = cs[c, low, h].astype(jnp.float32)
            for d in range(1, HIST):
                total = total + cr[c, low, lax.rem(h + d, HIST)].astype(jnp.float32)
            for part in range(2):
                out[0, part, pl.ds(low * 32, 32), lanes(c)] = total[:, part * LANES:(part + 1) * LANES]

    def prepare_masks():
        bound_copy.wait()
        row_ky = lax.broadcasted_iota(jnp.int32, (32, 256), 0)
        column = lax.broadcasted_iota(jnp.int32, (32, 256), 1)
        step = h * STEPS + column // 32
        for j in range(HIST):
            keep = (step < bbuf[j]) & (column % 32 == row_ky)
            masks[pl.ds(32 * j, 32), :] = jnp.where(keep, 1.0 / math.sqrt(STEPS * HIST), 0.0).astype(jnp.bfloat16)

    def prepare_advanced():
        adv_copy.wait()

        def one(t, carry):
            for part in range(2):
                rows[part] = abuf[part, :, :, lanes(t)].astype(jnp.float32).reshape(KDEV * STEPS, LANES)
            spot = pl.ds(pl.multiple_of(t * LANES, LANES), LANES)
            for low in range(2):
                for g in range(2):
                    pair = []
                    for part in range(2):
                        pieces = [rows[part, pl.ds(low * 256 + 4 * g + s, 32, STEPS), :] for s in range(4)]
                        pair.append(jnp.concatenate(pieces, axis=0).T)
                        bt[low, g, part, spot, :] = pair[part]
                    bt[low, g, 2, spot, :] = pair[0] + pair[1]
            return carry

        lax.fori_loop(0, CHUNKS, one, 0)

    coupling_load.wait()
    pair = cbuf[...].reshape(1, KDEV)
    own_c[...] = jnp.broadcast_to(jnp.concatenate([pair, pair], axis=1), (8, LANES))
    all_c[me] = own_c[...]
    tab_copy.wait()
    forward(0)
    pl.semaphore_wait(barrier, MOM - 1 + HIST - 1)
    exchange(s1, r1, s1_send, r1_recv, 0)
    for d in range(1, MOM):
        coupling_copy(other(me, d)).start()

    def send_ahead(c, carry):
        forward(c)
        exchange(s1, r1, s1_send, r1_recv, c)
        return carry

    lax.fori_loop(1, AHEAD, send_ahead, 0)
    prepare_masks()
    prepare_advanced()
    space_copy.wait()
    coupling_all().wait_recv()

    def step(i, carry):
        @pl.when(i < CHUNKS)
        def _():
            middle(i)
            exchange_back(i)

        @pl.when(i + AHEAD < CHUNKS)
        def _():
            send_ahead(i + AHEAD, 0)

        @pl.when((i >= BACK) & (i < CHUNKS + BACK))
        def _():
            for low in range(2):
                arrivals_back(i - BACK, low).wait_recv()
                products(i - BACK, low)

        @pl.when(i >= BACK + LAST)
        def _():
            finish(i - BACK - LAST)

        return carry

    lax.fori_loop(0, CHUNKS + BACK + LAST, step, 0)

    def drain(c, carry):
        arrivals(s1, r1, s1_send, r1_recv, c).wait_send()
        for low in range(2):
            arrivals_back(c, low).wait_send()
        for low in range(2):
            partial_all(c, low).wait_send()
        return carry

    coupling_all().wait_send()
    lax.fori_loop(0, CHUNKS, drain, 0)


def per_device(greens, advanced, coupling, bounds):
    tabs, space_tab = tables()
    any_spec = pl.BlockSpec(memory_space=pltpu.HBM)
    bf16, f32 = jnp.bfloat16, jnp.float32
    dma = pltpu.SemaphoreType.DMA
    blocks = pltpu.VMEM((CHUNKS, MOM, 64, LANES), bf16)
    parts = pltpu.VMEM((CHUNKS, 2, HIST, 32, 2 * LANES), bf16)
    return pl.pallas_call(
        kernel,
        out_shape=pltpu.VMEM((1, 2, KDEV, NO * NO), f32),
        in_specs=[any_spec] * 6,
        out_specs=pl.BlockSpec(memory_space=pltpu.VMEM),
        scratch_shapes=[
            pltpu.VMEM((CHUNKS, 2, STEPS, KDEV, LANES), bf16),
            pltpu.VMEM((2, KDEV, STEPS, NO * NO), bf16),
            pltpu.VMEM((3, 256, 256), bf16),
            pltpu.VMEM((512, 256), bf16),
            pltpu.SMEM((HIST,), jnp.int32),
            pltpu.VMEM((KDEV,), f32),
            pltpu.VMEM((8, LANES), f32),
            pltpu.VMEM((MOM, 8, LANES), f32),
            pltpu.VMEM((256, 256), bf16),
            blocks, blocks, blocks, blocks,
            pltpu.VMEM((2, KDEV * STEPS, LANES), f32),
            pltpu.VMEM((2, 2, 3, NO * NO, LANES), f32),
            pltpu.VMEM((2, 3, LANES, LANES), f32),
            pltpu.VMEM((2, 2, LANES, LANES), bf16),
            parts, parts,
            dma((CHUNKS,)), dma((5,)), dma, dma,
            dma((CHUNKS,)), dma((CHUNKS,)), dma((CHUNKS,)), dma((CHUNKS, 2)), dma((CHUNKS, 2)), dma((CHUNKS, 2)),
        ],
        compiler_params=pltpu.CompilerParams(collective_id=0, has_side_effects=True, vmem_limit_bytes=63 << 20),
    )(greens, advanced, coupling, bounds, jnp.asarray(tabs), jnp.asarray(space_tab))


def solution(mesh):
    in_specs = (P(None, "hist", "mom", None), P(None, "mom", "hist", None), P("mom"), P())
    out_specs = P("hist", None, "mom", None)
    return jax.shard_map(per_device, mesh=mesh, in_specs=in_specs, out_specs=out_specs, check_vma=False)
```

```python
import functools
import math

import jax
import jax.numpy as jnp
import ml_dtypes
import numpy as np
from jax import lax
from jax.experimental import pallas as pl
from jax.experimental.pallas import tpu as pltpu
from jax.sharding import PartitionSpec as P

MESH = pl.DeviceIdType.MESH
L = 32
NO = 32
LANES = 128
CHUNKS = 8
MOM = 16
HIST = 8
STEPS = 8
KDEV = 64
AHEAD = 4
BACK = 3
LAST = 2


def tables():
    index = np.arange(L, dtype=np.int32)
    phase = index[:, None] * index[None, :] % L
    angle = phase.astype(np.float32) * np.float32(2.0 * math.pi / L)
    norm = np.float32(1.0 / math.sqrt(L))
    cosines = (np.cos(angle) * norm).astype(ml_dtypes.bfloat16).astype(np.float32)
    sines = (np.sin(angle) * norm).astype(ml_dtypes.bfloat16).astype(np.float32)
    ahead = np.array([[cosines, -sines], [sines, cosines]])
    back = np.array([[cosines, sines], [-sines, cosines]])
    eye = np.eye(2, dtype=np.float32)
    group = np.array([[0, 16]] + [[m, L - m] for m in range(1, MOM)])
    flip = (-index) % L
    pairs = np.arange(L).reshape(MOM, 2)

    first = np.einsum("ridyk,st,lm->dsyrlitmk", ahead[:, :, group, :].reshape(2, 2, MOM, 2, L), eye, eye)
    along = ahead[:, :, :, pairs]
    space = np.einsum("rixdl,st,yw->rsyxdtwil", along, eye, eye)
    turned = along[:, :, flip]
    mirror = np.einsum("rixdl,st,yw->rsyxdtwil", turned, eye, eye[::-1])
    mirror_own = np.einsum("rixdl,st,yw->rsyxdtwil", turned, eye, eye)
    third = np.einsum("ridlx,st,yw->dlsyritwx", back[:, :, pairs, :], eye, eye)
    last = np.einsum("rikdy,st->rskdtyi", back[:, :, :, group], np.eye(4, dtype=np.float32))
    square = lambda a: a.reshape(256, 256)
    moved = [np.concatenate([square(space), square(m)]) for m in (mirror, mirror_own)]
    return (
        np.stack([square(first), square(third), square(last)]).astype(ml_dtypes.bfloat16),
        np.stack(moved).astype(ml_dtypes.bfloat16),
    )


def other(me, d):
    return lax.rem(me // 4 + d // 4, 4) * 4 + lax.rem(lax.rem(me, 4) + d % 4, 4)


def kernel(
    greens, advanced, coupling, bounds, tabs, space_tab, out,
    gbuf, abuf, tbuf, sbuf, bbuf, cbuf, own_c, all_c, masks,
    s1, r1, s2, r2, rows, bt, at, acc, cs, cr,
    in_sem, load_sem, c_send, c_recv, s1_send, r1_recv, s2_send, r2_recv, cs_send, cr_recv,
):
    me = lax.axis_index("mom")
    h = lax.axis_index("hist")

    def lanes(c):
        return pl.ds(pl.multiple_of(c * LANES, LANES), LANES)

    pick = jnp.where(me == 0, 1, 0)
    tab_copy = pltpu.make_async_copy(tabs, tbuf, load_sem.at[0])
    space_copy = pltpu.make_async_copy(space_tab.at[pick], sbuf, load_sem.at[1])
    adv_copy = pltpu.make_async_copy(advanced, abuf, load_sem.at[2])
    bound_copy = pltpu.make_async_copy(bounds, bbuf, load_sem.at[3])

    def green_copy(c):
        return pltpu.make_async_copy(greens.at[:, :, :, lanes(c)], gbuf.at[c], in_sem.at[c])

    barrier = pltpu.get_barrier_semaphore()
    for d in range(1, MOM):
        pl.semaphore_signal(barrier, inc=1, device_id=(other(me, d), h), device_id_type=MESH)
    for d in range(1, HIST):
        pl.semaphore_signal(barrier, inc=1, device_id=(me, lax.rem(h + d, HIST)), device_id_type=MESH)

    coupling_load = pltpu.make_async_copy(coupling, cbuf, load_sem.at[4])
    coupling_load.start()
    tab_copy.start()
    green_copy(0).start()
    green_copy(1).start()
    space_copy.start()
    bound_copy.start()

    for c in range(2, CHUNKS):
        green_copy(c).start()
    adv_copy.start()

    def exchange(src, dst, send, recv, c):
        for d in range(1, MOM):
            p = other(me, d)
            pltpu.make_async_remote_copy(
                src_ref=src.at[c, p], dst_ref=dst.at[c, me], send_sem=send.at[c], recv_sem=recv.at[c],
                device_id=(p, h), device_id_type=MESH,
            ).start()
        dst[c, me] = src[c, me]

    def exchange_back(c):
        for low in range(2):
            half = pl.ds(low * 32, 32)
            for d in range(1, MOM):
                p = other(me, d)
                pltpu.make_async_remote_copy(
                    src_ref=s2.at[c, p, half], dst_ref=r2.at[c, me, half],
                    send_sem=s2_send.at[c], recv_sem=r2_recv.at[c, low],
                    device_id=(p, h), device_id_type=MESH,
                ).start()
        r2[c, me] = s2[c, me]

    def arrivals_back(c, low):
        half = pl.ds(low * 32, 32)
        return pltpu.make_async_remote_copy(
            src_ref=s2.at[c, pl.ds(0, MOM - 1), half], dst_ref=r2.at[c, pl.ds(0, MOM - 1), half],
            send_sem=s2_send.at[c], recv_sem=r2_recv.at[c, low], device_id=(other(me, 1), h), device_id_type=MESH,
        )

    def arrivals(src, dst, send, recv, c):
        return pltpu.make_async_remote_copy(
            src_ref=src.at[c, pl.ds(0, MOM - 1)], dst_ref=dst.at[c, pl.ds(0, MOM - 1)],
            send_sem=send.at[c], recv_sem=recv.at[c], device_id=(other(me, 1), h), device_id_type=MESH,
        )

    def coupling_copy(p):
        return pltpu.make_async_remote_copy(
            src_ref=own_c, dst_ref=all_c.at[me], send_sem=c_send, recv_sem=c_recv,
            device_id=(p, h), device_id_type=MESH,
        )

    def coupling_all():
        return pltpu.make_async_remote_copy(
            src_ref=all_c.at[pl.ds(0, MOM - 1)], dst_ref=all_c.at[pl.ds(0, MOM - 1)], send_sem=c_send, recv_sem=c_recv,
            device_id=(other(me, 1), h), device_id_type=MESH,
        )

    def partial_all(c, low):
        return pltpu.make_async_remote_copy(
            src_ref=cs.at[c, low, pl.ds(0, HIST - 1)], dst_ref=cr.at[c, low, pl.ds(0, HIST - 1)],
            send_sem=cs_send.at[c, low], recv_sem=cr_recv.at[c, low], device_id=(me, lax.rem(h + 1, HIST)), device_id_type=MESH,
        )

    def two(load, q):
        return jnp.concatenate([load(2 * q), load(2 * q + 1)], axis=1)

    def spread(dst, c, q, value):
        value = value.astype(jnp.bfloat16)
        for n in range(2):
            part = value[:, n * LANES:(n + 1) * LANES].reshape(MOM, 16, LANES)
            dst[c, :, pl.ds((2 * q + n) * 16, 16), :] = part

    def gathered(src, c, first=0):
        return lambda g: src[c, :, pl.ds(first + g * 16, 16), :].reshape(256, LANES)

    def forward(c):
        green_copy(c).wait()
        for q in range(2):
            data = two(lambda g: gbuf[c, :, pl.ds(2 * g, 2)].reshape(256, LANES), q)
            spread(s1, c, q, jnp.dot(tbuf[0], data, preferred_element_type=jnp.float32))

    def middle(c):
        arrivals(s1, r1, s1_send, r1_recv, c).wait_recv()
        low = lax.broadcasted_iota(jnp.int32, (1, LANES), 1) < LANES // 2
        weight = jnp.where(low, all_c[2 * c, 0:1, :], all_c[2 * c + 1, 0:1, :])
        weight = weight * weight
        weight = jnp.concatenate([weight, weight], axis=1)
        for q in range(2):
            data = two(gathered(r1, c), q)
            space = jnp.dot(sbuf[...], data, preferred_element_type=jnp.float32)
            re, im, mre, mim = (space[n * 128:(n + 1) * 128] for n in range(4))
            square_re = re * re - im * im
            square_im = 2.0 * re * im
            sigma_re = weight * (square_re * mre + square_im * mim)
            sigma_im = weight * (square_im * mre - square_re * mim)
            sigma = jnp.concatenate([sigma_re.astype(jnp.bfloat16), sigma_im.astype(jnp.bfloat16)], axis=0)
            value = jnp.dot(tbuf[1], sigma, preferred_element_type=jnp.float32).reshape(MOM, 2, 8, 2 * LANES)
            value = jnp.concatenate([value[..., :LANES], value[..., LANES:]], axis=2).astype(jnp.bfloat16)
            for low in range(2):
                s2[c, :, pl.ds(low * 32 + q * 16, 16), :] = value[:, low]

    def products(c, low):
        final = jnp.dot(tbuf[2], two(gathered(r2, c, low * 32), 0), preferred_element_type=jnp.float32)
        for g in range(2):
            re = final[:128, g * LANES:(g + 1) * LANES].T
            im = final[128:, g * LANES:(g + 1) * LANES].T
            at[g, 0] = re
            at[g, 1] = im
            at[g, 2] = re + im

        def one_block(n, carry):
            g, first = n // 2, n % 2 * (2 * NO)

            def one_orbital(m, sums):
                b = [bt[low, g, part, pl.ds(pl.multiple_of(m * NO, NO), NO), :] for part in range(3)]
                result = []
                for a in range(2):
                    for part in range(3):
                        factor = at[g, part, pl.ds(first + a * NO + m, 1), :]
                        result.append(sums[3 * a + part] + factor * b[part])
                return tuple(result)

            zero = jnp.zeros((NO, LANES), jnp.float32)
            sums = lax.fori_loop(0, NO, one_orbital, (zero,) * 6, unroll=32)
            for a in range(2):
                re_re, im_im, both = sums[3 * a:3 * a + 3]
                spot = pl.ds(first + a * NO, NO)
                acc[g, 0, spot, :] = (re_re - im_im).astype(jnp.bfloat16)
                acc[g, 1, spot, :] = (both - (re_re + im_im)).astype(jnp.bfloat16)
            return carry

        for n in range(4):
            one_block(n, 0)
        terms = jnp.concatenate([acc[g].reshape(2 * LANES, LANES) for g in range(2)], axis=1)
        sums = lax.dot_general(masks[...], terms, (((1,), (1,)), ((), ())), preferred_element_type=jnp.float32)
        cs[c, low] = sums.astype(jnp.bfloat16).reshape(HIST, 32, 2 * LANES)
        for d in (4, 5, 3, 2, 6, 7, 1):
            p = lax.rem(h + d, HIST)
            pltpu.make_async_remote_copy(
                src_ref=cs.at[c, low, p], dst_ref=cr.at[c, low, h],
                send_sem=cs_send.at[c, low], recv_sem=cr_recv.at[c, low],
                device_id=(me, p), device_id_type=MESH,
            ).start()

    def finish(c):
        for low in range(2):
            partial_all(c, low).wait_recv()
            total = cs[c, low, h].astype(jnp.float32)
            for d in range(1, HIST):
                total = total + cr[c, low, lax.rem(h + d, HIST)].astype(jnp.float32)
            for part in range(2):
                out[0, part, pl.ds(low * 32, 32), lanes(c)] = total[:, part * LANES:(part + 1) * LANES]

    def prepare_masks():
        bound_copy.wait()
        row_ky = lax.broadcasted_iota(jnp.int32, (32, 256), 0)
        column = lax.broadcasted_iota(jnp.int32, (32, 256), 1)
        step = h * STEPS + column // 32
        for j in range(HIST):
            keep = (step < bbuf[j]) & (column % 32 == row_ky)
            masks[pl.ds(32 * j, 32), :] = jnp.where(keep, 1.0 / math.sqrt(STEPS * HIST), 0.0).astype(jnp.bfloat16)

    def prepare_advanced():
        adv_copy.wait()

        def one(t, carry):
            for part in range(2):
                rows[part, pl.ds(0, KDEV * STEPS), :] = abuf[part, :, :, lanes(t)].astype(jnp.float32).reshape(KDEV * STEPS, LANES)
            spot = pl.ds(pl.multiple_of(t * LANES, LANES), LANES)
            for low in range(2):
                for g in range(2):
                    pair = []
                    for part in range(2):
                        pieces = [rows[part, pl.ds(low * 256 + 4 * g + s, 32, STEPS), :] for s in range(4)]
                        pair.append(jnp.concatenate(pieces, axis=0).T)
                        bt[low, g, part, spot, :] = pair[part]
                    bt[low, g, 2, spot, :] = pair[0] + pair[1]
            return carry

        lax.fori_loop(0, CHUNKS, one, 0)

    coupling_load.wait()
    pair = cbuf[...].reshape(1, KDEV)
    own_c[...] = jnp.broadcast_to(jnp.concatenate([pair, pair], axis=1), (8, LANES))
    all_c[me] = own_c[...]
    tab_copy.wait()
    forward(0)
    pl.semaphore_wait(barrier, MOM - 1 + HIST - 1)
    exchange(s1, r1, s1_send, r1_recv, 0)
    for d in range(1, MOM):
        coupling_copy(other(me, d)).start()

    def send_ahead(c, carry):
        forward(c)
        exchange(s1, r1, s1_send, r1_recv, c)
        return carry

    lax.fori_loop(1, AHEAD, send_ahead, 0)
    prepare_masks()
    prepare_advanced()
    space_copy.wait()
    coupling_all().wait_recv()

    def step(i, carry):
        @pl.when(i < CHUNKS)
        def _():
            middle(i)
            exchange_back(i)

        @pl.when(i + AHEAD < CHUNKS)
        def _():
            send_ahead(i + AHEAD, 0)

        @pl.when((i >= BACK) & (i < CHUNKS + BACK))
        def _():
            for low in range(2):
                arrivals_back(i - BACK, low).wait_recv()
                products(i - BACK, low)

        @pl.when(i >= BACK + LAST)
        def _():
            finish(i - BACK - LAST)

        return carry

    lax.fori_loop(0, CHUNKS + BACK + LAST, step, 0)

    def drain(c, carry):
        arrivals(s1, r1, s1_send, r1_recv, c).wait_send()
        for low in range(2):
            arrivals_back(c, low).wait_send()
        for low in range(2):
            partial_all(c, low).wait_send()
        return carry

    coupling_all().wait_send()
    lax.fori_loop(0, CHUNKS, drain, 0)


def per_device(greens, advanced, coupling, bounds):
    tabs, space_tab = tables()
    any_spec = pl.BlockSpec(memory_space=pltpu.HBM)
    bf16, f32 = jnp.bfloat16, jnp.float32
    dma = pltpu.SemaphoreType.DMA
    blocks = pltpu.VMEM((CHUNKS, MOM, 64, LANES), bf16)
    parts = pltpu.VMEM((CHUNKS, 2, HIST, 32, 2 * LANES), bf16)
    return pl.pallas_call(
        kernel,
        out_shape=pltpu.VMEM((1, 2, KDEV, NO * NO), f32),
        in_specs=[any_spec] * 6,
        out_specs=pl.BlockSpec(memory_space=pltpu.VMEM),
        scratch_shapes=[
            pltpu.VMEM((CHUNKS, 2, STEPS, KDEV, LANES), bf16),
            pltpu.VMEM((2, KDEV, STEPS, NO * NO), bf16),
            pltpu.VMEM((3, 256, 256), bf16),
            pltpu.VMEM((512, 256), bf16),
            pltpu.SMEM((HIST,), jnp.int32),
            pltpu.VMEM((KDEV,), f32),
            pltpu.VMEM((8, LANES), f32),
            pltpu.VMEM((MOM, 8, LANES), f32),
            pltpu.VMEM((256, 256), bf16),
            blocks, blocks, blocks, blocks,
            pltpu.VMEM((2, KDEV * STEPS + 8, LANES), f32),
            pltpu.VMEM((2, 2, 3, NO * NO, LANES), f32),
            pltpu.VMEM((2, 3, LANES, LANES), f32),
            pltpu.VMEM((2, 2, LANES, LANES), bf16),
            parts, parts,
            dma((CHUNKS,)), dma((5,)), dma, dma,
            dma((CHUNKS,)), dma((CHUNKS,)), dma((CHUNKS,)), dma((CHUNKS, 2)), dma((CHUNKS, 2)), dma((CHUNKS, 2)),
        ],
        compiler_params=pltpu.CompilerParams(collective_id=0, has_side_effects=True, vmem_limit_bytes=63 << 20),
    )(greens, advanced, coupling, bounds, jnp.asarray(tabs), jnp.asarray(space_tab))


def solution(mesh):
    in_specs = (P(None, "hist", "mom", None), P(None, "mom", "hist", None), P("mom"), P())
    out_specs = P("hist", None, "mom", None)
    return jax.shard_map(per_device, mesh=mesh, in_specs=in_specs, out_specs=out_specs, check_vma=False)
```
